1024 devices in a mesh: dom: 64 (over x, z_lo, core), grp: 16 (over y, z_hi).
Axes of the slice: x: 4, y: 4, z: 32 (z_hi: 4, z_lo: 8; z = z_hi * 8 + z_lo), core: 2. Of those that a mesh axis runs over, the one named last changes fastest.
Arguments:
- orbitals: float32 [512, 384, 512], P('grp', 'dom'), may hold values from -10 to 10, as said below
- potential: float32 [384, 512], P('dom'), may hold values from -2 to 2
Outputs:
- filtered: float32 [512, 384, 512], P('grp', 'dom')
- correlation: float32 [512, 512], P('grp', 'dom')
The draws below stay inside these ranges and needn't reach their ends.
Inputs may be any that keep to these rules, and one draw needn't show every extreme that they name: `orbitals`: entries of order one.
All inputs are finite; a program needn't handle non-finite values.
Results may differ from the reference program's by a relative error of at most 0.003.
Values may be sent and summed in bfloat16 or wider, within the bound.
A program may use at most 32 MiB of HBM per device.

```python
import jax
import jax.numpy as jnp
from jax import lax

ORBS = 512
NX = 32
NY = 16
NPLANE = 512
NZ = 384
NCELLS = 196608


def draw_orbitals(key, part):
    keys = jax.random.split(key, 5)
    noise = jax.random.normal(keys[0], (ORBS, NZ, NPLANE), jnp.float32)
    first_amp = 0.6 * jax.random.normal(keys[1], (ORBS, 1, 1), jnp.float32)
    second_amp = 0.6 * jax.random.normal(keys[2], (ORBS, 1, 1), jnp.float32)
    first_field = jax.random.normal(keys[3], (1, NZ, NPLANE), jnp.float32)
    second_field = jax.random.normal(keys[4], (1, NZ, NPLANE), jnp.float32)
    values = noise + first_amp * first_field + second_amp * second_field
    return jnp.clip(values, -10.0, 10.0)


def block_scale(rng, shape, cuts, smallest, high):
    def one(dim, blocks):
        draws = jax.random.uniform(jax.random.fold_in(jax.random.fold_in(rng, 6), dim), (blocks,), jnp.float32, smallest / len(cuts), high / len(cuts))
        return jnp.repeat(jnp.exp(draws), shape[dim] // blocks).reshape((-1,) + (1,) * (len(shape) - dim - 1))

    factor_of = one(*cuts[0])
    for cut in cuts[1:]:
        factor_of = factor_of * one(*cut)
    return factor_of


def setup_inputs(seed: int = 0) -> dict:
    key_list = jax.random.split(jax.random.key(seed), 3)
    orbitals = draw_orbitals(jax.random.fold_in(key_list[2], 71), 0)
    potential = jnp.clip(jax.random.uniform(key_list[1], (NZ, NPLANE), jnp.float32, -2.0, 2.0) * block_scale(key_list[1], (NZ, NPLANE), ((0, 64),), -0.4, 0.0), -2.0, 2.0)
    return dict(orbitals=orbitals, potential=potential)


COEFFS = [-5369.0 / 1800.0, 12.0 / 7.0, -15.0 / 56.0, 10.0 / 189.0, -1.0 / 112.0, 2.0 / 1925.0, -1.0 / 16632.0]
CENTER = 13.0
HALF_WIDTH = 11.0


def hamiltonian(block, potential):
    laplace = 3.0 * COEFFS[0] * block
    for reach in range(1, 7):
        for axis_num in (1, 2, 3):
            laplace = laplace + COEFFS[reach] * (jnp.roll(block, reach, axis_num) + jnp.roll(block, -reach, axis_num))
    return -0.5 / 0.25 * laplace + potential[None] * block


def filter_block(block, potential):
    previous = block
    current = (hamiltonian(block, potential) - CENTER * block) / HALF_WIDTH
    for degree in range(3):
        following = 2.0 * (hamiltonian(current, potential) - CENTER * current) / HALF_WIDTH - previous
        previous = current
        current = following
    return current


def reference(orbitals, potential):
    planes = orbitals.shape[1]
    shaped = orbitals.reshape((ORBS // 16, 16, planes, NY, NX))
    field = potential.reshape((planes, NY, NX))
    filtered = lax.map(lambda block: filter_block(block, field), shaped).reshape(orbitals.shape)
    rounded = filtered.astype(jnp.bfloat16)
    flat = rounded.reshape(ORBS, -1).astype(jnp.float32)
    correlation = jnp.dot(flat, flat.T, precision=lax.Precision.HIGHEST, preferred_element_type=jnp.float32) / NCELLS
    return filtered, correlation
```

```python
import jax
import jax.numpy as jnp
import ml_dtypes
import numpy as np
from jax import lax
from jax.experimental import pallas as pl
from jax.experimental.pallas import tpu as pltpu
from jax.sharding import PartitionSpec as P

NX = 32
NY = 16
CELLS = NX * NY
NZ = 384
CORES = 2
CHUNKS = 2
ROWS = 16
LANES = 128
PLANES = 6

COEFFS = [
    -5369.0 / 1800.0,
    12.0 / 7.0,
    -15.0 / 56.0,
    10.0 / 189.0,
    -1.0 / 112.0,
    2.0 / 1925.0,
    -1.0 / 16632.0,
]
CENTER = 13.0
HALF_WIDTH = 11.0
KINETIC = -0.5 / 0.25

HIGH_AT = [1, 2, 3, 4, 5, 6]
LOW_AT = [0, 8, 9, 10, 11, 7]


def plane_stencil():
    cells = np.arange(CELLS)
    row_of, col_of = cells // NX, cells % NX
    row_gap = (row_of[:, None] - row_of[None, :]) % NY
    col_gap = (col_of[:, None] - col_of[None, :]) % NX
    stencil = np.zeros((CELLS, CELLS), np.float64)
    for reach in range(1, 7):
        rows = (col_gap == 0) & ((row_gap == reach) | (row_gap == NY - reach))
        cols = (row_gap == 0) & ((col_gap == reach) | (col_gap == NX - reach))
        stencil += COEFFS[reach] / COEFFS[1] * (rows.astype(np.float64) + cols.astype(np.float64))
    return stencil.astype(ml_dtypes.bfloat16)


def make_kernel(xs, zls, ys, zhs):
    doms = xs * zls * CORES

    def kernel(
        v_hbm, pot_hbm, sten_hbm, out_hbm, corr_ref,
        buf_a, buf_b, sten, pot, diag, sbuf, from_left, from_right,
        rounded, relay, gathered, parts, got_x, sum_x, got_zl, sum_zl, got_zh,
        load_sem, store_sem, halo_send, halo_recv, z_send, z_recv, relay_recv, relay_send,
        y_send, y_recv, x_send, x_recv, zl_send, zl_recv, zh_send, zh_recv,
    ):
        dom = lax.axis_index("dom")
        grp = lax.axis_index("grp")
        core = lax.rem(dom, CORES)
        zl = lax.rem(dom // CORES, zls)
        x = dom // (CORES * zls)
        zh = lax.rem(grp, zhs)
        y = grp // zhs

        def at(x_=x, zl_=zl, core_=core, y_=y, zh_=zh):
            return {"dom": (x_ * zls + zl_) * CORES + core_, "grp": y_ * zhs + zh_}

        def shift(value, by, count):
            return lax.rem(value + (by + count), count)

        def send(src, dst, send_sem, recv_sem, device):
            copy = pltpu.make_async_remote_copy(
                src_ref=src, dst_ref=dst, send_sem=send_sem, recv_sem=recv_sem,
                device_id=device, device_id_type=pl.DeviceIdType.MESH,
            )
            copy.start()
            return copy

        left = {"dom": shift(dom, -1, doms), "grp": grp}
        right = {"dom": shift(dom, 1, doms), "grp": grp}
        x_peers = [(o, c) for o in range(xs) for c in range(CORES) if (o, c) != (0, 0)]

        def x_peer(off, flip):
            return at(x_=shift(x, off, xs), core_=lax.rem(core + flip, CORES))

        loads = []
        for c in range(CHUNKS):
            copy = pltpu.make_async_copy(
                v_hbm.at[:, pl.ds(c * ROWS, ROWS), :], buf_a.at[c], load_sem.at[c]
            )
            copy.start()
            loads.append(copy)
        pot_load = pltpu.make_async_copy(pot_hbm, pot, load_sem.at[2])
        pot_load.start()
        sten_load = pltpu.make_async_copy(sten_hbm, sten, load_sem.at[3])
        sten_load.start()

        barrier = pltpu.get_barrier_semaphore()
        peers = [left, right]
        peers += [at(zh_=shift(zh, o, zhs)) for o in range(1, zhs)]
        peers += [at(y_=shift(y, o, ys)) for o in range(1, ys)]
        peers += [x_peer(o, c) for o, c in x_peers]
        peers += [at(zl_=shift(zl, o, zls)) for o in range(1, zls)]
        for peer in peers:
            pl.semaphore_signal(barrier, inc=1, device_id=peer, device_id_type=pl.DeviceIdType.MESH)

        bufs = [buf_a, buf_b]

        def split_store(s, c, plane, lanes, value):
            high = value.astype(jnp.bfloat16)
            low = (value - high.astype(jnp.float32)).astype(jnp.bfloat16)
            sbuf[s, c, HIGH_AT[plane], :, lanes] = high
            sbuf[s, c, LOW_AT[plane], :, lanes] = low

        def local_part(s, c):
            cur, nxt = bufs[s % 2], bufs[(s + 1) % 2]
            scale = (1.0 if s == 0 else 2.0) / HALF_WIDTH
            couple = [scale * KINETIC * k for k in COEFFS]
            lhs = sbuf[s, c].reshape(12 * ROWS, CELLS)
            for half in range(2):
                wide = pl.ds(half * 256, 256)
                res = jnp.dot(lhs, sten[:, wide], preferred_element_type=jnp.float32)
                res = res.reshape(12, ROWS, 256)
                for part in range(2):
                    lanes = pl.ds(half * 256 + part * LANES, LANES)
                    own = [cur[c, p, :, lanes] for p in range(PLANES)]
                    for p in range(PLANES):
                        flat = (res[HIGH_AT[p]] + res[LOW_AT[p]])[:, part * LANES : (part + 1) * LANES]
                        total = couple[1] * flat + (scale * diag[pl.ds(p, 1), lanes]) * own[p]
                        for k in range(1, PLANES):
                            if p - k >= 0 and p + k < PLANES:
                                total += couple[k] * (own[p - k] + own[p + k])
                            elif p - k >= 0:
                                total += couple[k] * own[p - k]
                            elif p + k < PLANES:
                                total += couple[k] * own[p + k]
                        if s > 0:
                            total -= nxt[c, p, :, lanes]
                        nxt[c, p, :, lanes] = total

        def finish(s, c, lanes):
            nxt = bufs[(s + 1) % 2]
            scale = (1.0 if s == 0 else 2.0) / HALF_WIDTH
            couple = [scale * KINETIC * k for k in COEFFS]
            lower = [from_left[s, c, i, :, lanes].astype(jnp.float32) for i in range(7)]
            lower[5] = lower[5] + lower[6]
            upper = [from_right[s, c, i, :, lanes].astype(jnp.float32) for i in range(7)]
            upper = [upper[1] + upper[0]] + upper[2:]
            results = []
            for p in range(PLANES):
                total = nxt[c, p, :, lanes]
                for i in range(p, PLANES):
                    total += couple[p + 6 - i] * lower[i]
                for i in range(p + 1):
                    total += couple[6 + i - p] * upper[i]
                nxt[c, p, :, lanes] = total
                results.append(total)
            return results

        def send_halo(s, c):
            return [
                send(sbuf.at[s, c, pl.ds(0, 7)], from_right.at[s, c], halo_send.at[s, c, 0], halo_recv.at[s, c, 0], left),
                send(sbuf.at[s, c, pl.ds(1, 7)], from_left.at[s, c], halo_send.at[s, c, 1], halo_recv.at[s, c, 1], right),
            ]

        for c in range(CHUNKS):
            loads[c].wait()
            for q in range(CELLS // LANES):
                lanes = pl.ds(q * LANES, LANES)
                for p in range(PLANES):
                    split_store(0, c, p, lanes, buf_a[c, p, :, lanes])
        pot_load.wait()
        diag[...] = pot[...] + (3.0 * KINETIC * COEFFS[0] - CENTER)
        sten_load.wait()
        local_part(0, 0)
        pl.semaphore_wait(barrier, len(peers))
        halos = {}
        for c in range(CHUNKS):
            halos[0, c] = send_halo(0, c)
        for c in range(1, CHUNKS):
            local_part(0, c)

        zh_up, zh_down, zh_far = shift(zh, 1, zhs), shift(zh, -1, zhs), shift(zh, 2, zhs)
        sends = []
        stores = []
        arrivals = {}
        relays = {}
        y_arrivals = []

        def spread_y(c, rel, source):
            for o in range(1, ys):
                copy = send(
                    gathered.at[y, source, c], gathered.at[y, source, c],
                    y_send.at[c, rel, o - 1], y_recv.at[c, rel, o - 1], at(y_=shift(y, o, ys)),
                )
                sends.append(copy)
                y_arrivals.append(copy)

        for s in range(4):
            last = s == 3
            for c in range(CHUNKS):
                for copy in halos[s, c]:
                    copy.wait_recv()
                for q in range(CELLS // LANES):
                    lanes = pl.ds(q * LANES, LANES)
                    results = finish(s, c, lanes)
                    for p, value in enumerate(results):
                        if last:
                            rounded[c, q, p // 2, :, pl.ds((p % 2) * LANES, LANES)] = value.astype(jnp.bfloat16)
                        else:
                            split_store(s + 1, c, p, lanes, value)
                if not last:
                    halos[s + 1, c] = send_halo(s + 1, c)
                    local_part(s + 1, c)
                    continue
                first, other = (zh_up, zh_down) if c == 0 else (zh_down, zh_up)
                relays[c] = send(rounded.at[c, zh_far], relay.at[c], z_send.at[c, 2], relay_recv.at[c], at(zh_=first))
                arrivals[c, 0] = send(rounded.at[c, first], gathered.at[y, zh, c], z_send.at[c, 0], z_recv.at[c, 0], at(zh_=first))
                arrivals[c, 1] = send(rounded.at[c, other], gathered.at[y, zh, c], z_send.at[c, 1], z_recv.at[c, 1], at(zh_=other))
                gathered[y, zh, c] = rounded[c, zh]
                spread_y(c, 0, zh)
                copy = pltpu.make_async_copy(
                    buf_a.at[c], out_hbm.at[:, pl.ds(c * ROWS, ROWS), :], store_sem.at[c]
                )
                copy.start()
                stores.append(copy)

        for c in range(CHUNKS):
            first, other = (zh_up, zh_down) if c == 0 else (zh_down, zh_up)
            relays[c].wait_recv()
            arrivals[c, 2] = send(relay.at[c], gathered.at[y, other, c], relay_send.at[c], z_recv.at[c, 2], at(zh_=first))
            arrivals[c, 0].wait_recv()
            spread_y(c, 1, other)
            arrivals[c, 1].wait_recv()
            spread_y(c, 2, first)
        for c in range(CHUNKS):
            arrivals[c, 2].wait_recv()
            spread_y(c, 3, zh_far)
        for copy in y_arrivals:
            copy.wait_recv()

        own_rows = zhs * CHUNKS * ROWS
        x_arrivals = []
        for off in (2, 1, 3, 0):
            dest = shift(x, off, xs)
            total = jnp.zeros((own_rows, own_rows), jnp.float32)
            for i in range(PLANES // 2):
                total += lax.dot_general(
                    gathered[dest, :, :, i].reshape(own_rows, 2 * LANES),
                    gathered[y, :, :, i].reshape(own_rows, 2 * LANES),
                    (((1,), (1,)), ((), ())),
                    preferred_element_type=jnp.float32,
                )
            total = total.reshape(zls, CORES, 8, own_rows)
            for b in range(CORES):
                parts[off, b] = total[:, b]
            for flip in range(CORES):
                if (off, flip) == (0, 0):
                    continue
                copy = send(
                    parts.at[off, lax.rem(core + flip, CORES)], got_x.at[off, flip],
                    x_send.at[off, flip], x_recv.at[off, flip], x_peer(off, flip),
                )
                sends.append(copy)
                x_arrivals.append((off, flip, copy))
        total = parts[0, core]
        for off, flip, copy in x_arrivals:
            copy.wait_recv()
            total += got_x[off, flip]
        sum_x[...] = total

        zl_arrivals = []
        for o in range(1, zls):
            dest = shift(zl, o, zls)
            copy = send(sum_x.at[dest], got_zl.at[o], zl_send.at[o], zl_recv.at[o], at(zl_=dest))
            sends.append(copy)
            zl_arrivals.append(copy)
        total = sum_x[zl]
        for o, copy in enumerate(zl_arrivals):
            copy.wait_recv()
            total += got_zl[o + 1]
        sum_zl[...] = total

        zh_arrivals = []
        for o in range(1, zhs):
            dest = shift(zh, o, zhs)
            copy = send(sum_zl, got_zh.at[o], zh_send.at[o], zh_recv.at[o], at(zh_=dest))
            sends.append(copy)
            zh_arrivals.append(copy)
        for o, copy in enumerate(zh_arrivals):
            copy.wait_recv()
            total += got_zh[o + 1]
        width = CHUNKS * ROWS
        mine = jnp.zeros((8, width), jnp.float32)
        for o in range(zhs):
            mine = jnp.where(zh == o, total[:, o * width : (o + 1) * width], mine)
        corr_ref[...] = mine * (1.0 / (NZ * CELLS))

        for s in range(4):
            for c in range(CHUNKS):
                for copy in halos[s, c]:
                    copy.wait_send()
        for copy in list(relays.values()) + list(arrivals.values()) + sends:
            copy.wait_send()
        for copy in stores:
            copy.wait()

    return kernel


def solution(mesh):
    zls, zhs = 8, 4
    xs = mesh.shape["dom"] // (zls * CORES)
    ys = mesh.shape["grp"] // zhs
    stencil = plane_stencil()

    def shards(orbitals, potential):
        planes = jnp.transpose(orbitals, (1, 0, 2))
        count = planes.shape[1]
        dma = pltpu.SemaphoreType.DMA
        f32, bf16 = jnp.float32, jnp.bfloat16
        filtered, corr = pl.pallas_call(
            make_kernel(xs, zls, ys, zhs),
            out_shape=(
                jax.ShapeDtypeStruct((PLANES, count, CELLS), f32),
                jax.ShapeDtypeStruct((8, count), f32),
            ),
            in_specs=[pl.BlockSpec(memory_space=pl.ANY)] * 3,
            out_specs=(
                pl.BlockSpec(memory_space=pl.ANY),
                pl.BlockSpec(memory_space=pltpu.VMEM),
            ),
            scratch_shapes=[
                pltpu.VMEM((CHUNKS, PLANES, ROWS, CELLS), f32),
                pltpu.VMEM((CHUNKS, PLANES, ROWS, CELLS), f32),
                pltpu.VMEM((CELLS, CELLS), bf16),
                pltpu.VMEM((PLANES, CELLS), f32),
                pltpu.VMEM((PLANES, CELLS), f32),
                pltpu.VMEM((4, CHUNKS, 12, ROWS, CELLS), bf16),
                pltpu.VMEM((4, CHUNKS, 7, ROWS, CELLS), bf16),
                pltpu.VMEM((4, CHUNKS, 7, ROWS, CELLS), bf16),
                pltpu.VMEM((CHUNKS, zhs, 3, ROWS, 2 * LANES), bf16),
                pltpu.VMEM((CHUNKS, 3, ROWS, 2 * LANES), bf16),
                pltpu.VMEM((ys, zhs, CHUNKS, 3, ROWS, 2 * LANES), bf16),
                pltpu.VMEM((xs, CORES, zls, 8, LANES), f32),
                pltpu.VMEM((xs, CORES, zls, 8, LANES), f32),
                pltpu.VMEM((zls, 8, LANES), f32),
                pltpu.VMEM((zls, 8, LANES), f32),
                pltpu.VMEM((8, LANES), f32),
                pltpu.VMEM((zhs, 8, LANES), f32),
                dma((4,)),
                dma((CHUNKS,)),
                dma((4, CHUNKS, 2)),
                dma((4, CHUNKS, 2)),
                dma((CHUNKS, 3)),
                dma((CHUNKS, 3)),
                dma((CHUNKS,)),
                dma((CHUNKS,)),
                dma((CHUNKS, 4, 3)),
                dma((CHUNKS, 4, 3)),
                dma((xs, CORES)),
                dma((xs, CORES)),
                dma((zls,)),
                dma((zls,)),
                dma((zhs,)),
                dma((zhs,)),
            ],
            compiler_params=pltpu.CompilerParams(
                collective_id=0, has_side_effects=True, vmem_limit_bytes=40 * 1024 * 1024
            ),
            cost_estimate=pl.CostEstimate(flops=10**9, bytes_accessed=1500000, transcendentals=0),
        )(planes, potential, jnp.asarray(stencil))
        return jnp.transpose(filtered, (1, 0, 2)), jnp.transpose(corr, (1, 0))

    in_specs = (P("grp", "dom", None), P("dom", None))
    out_specs = (P("grp", "dom", None), P("grp", "dom"))
    return jax.shard_map(shards, mesh=mesh, in_specs=in_specs, out_specs=out_specs, check_vma=False)
```

```python
import jax
import jax.numpy as jnp
import ml_dtypes
import numpy as np
from jax import lax
from jax.experimental import pallas as pl
from jax.experimental.pallas import tpu as pltpu
from jax.sharding import PartitionSpec as P

NX = 32
NY = 16
CELLS = NX * NY
NZ = 384
CORES = 2
CHUNKS = 2
ROWS = 16
LANES = 128
PLANES = 6
PIECES = 2
PIECE = CELLS // PIECES
ROUNDS = 7

COEFFS = [
    -5369.0 / 1800.0,
    12.0 / 7.0,
    -15.0 / 56.0,
    10.0 / 189.0,
    -1.0 / 112.0,
    2.0 / 1925.0,
    -1.0 / 16632.0,
]
CENTER = 13.0
HALF_WIDTH = 11.0
KINETIC = -0.5 / 0.25

HIGH_AT = [1, 2, 3, 4, 5, 6]
LOW_AT = [0, 8, 9, 10, 11, 7]


def plane_stencil():
    cells = np.arange(CELLS)
    row_of, col_of = cells // NX, cells % NX
    row_gap = (row_of[:, None] - row_of[None, :]) % NY
    col_gap = (col_of[:, None] - col_of[None, :]) % NX
    stencil = np.zeros((CELLS, CELLS), np.float64)
    for reach in range(1, 7):
        rows = (col_gap == 0) & ((row_gap == reach) | (row_gap == NY - reach))
        cols = (row_gap == 0) & ((col_gap == reach) | (col_gap == NX - reach))
        stencil += COEFFS[reach] / COEFFS[1] * (rows.astype(np.float64) + cols.astype(np.float64))
    return stencil.astype(ml_dtypes.bfloat16)


def make_kernel(xs, zls, ys, zhs):
    doms = xs * zls * CORES

    def kernel(
        v_hbm, pot_hbm, sten_hbm, out_hbm, corr_ref,
        buf_a, buf_b, sten, pot, diag, sbuf, from_left, from_right,
        rounded, relay, gathered, parts, got_x, sum_x, got_zl, sum_zl, got_zh,
        load_sem, store_sem, token_up, token_down, halo_send, halo_recv, z_send, z_recv, relay_recv, relay_send,
        y_send, y_recv, x_send, x_recv, zl_send, zl_recv, zh_send, zh_recv,
    ):
        dom = lax.axis_index("dom")
        grp = lax.axis_index("grp")
        core = lax.rem(dom, CORES)
        zl = lax.rem(dom // CORES, zls)
        x = dom // (CORES * zls)
        zh = lax.rem(grp, zhs)
        y = grp // zhs

        def at(x_=x, zl_=zl, core_=core, y_=y, zh_=zh):
            return {"dom": (x_ * zls + zl_) * CORES + core_, "grp": y_ * zhs + zh_}

        def shift(value, by, count):
            return lax.rem(value + (by + count), count)

        def send(src, dst, send_sem, recv_sem, device):
            copy = pltpu.make_async_remote_copy(
                src_ref=src, dst_ref=dst, send_sem=send_sem, recv_sem=recv_sem,
                device_id=device, device_id_type=pl.DeviceIdType.MESH,
            )
            copy.start()
            return copy

        left = {"dom": shift(dom, -1, doms), "grp": grp}
        right = {"dom": shift(dom, 1, doms), "grp": grp}
        x_peers = [(o, c) for o in range(xs) for c in range(CORES) if (o, c) != (0, 0)]

        def x_peer(off, flip):
            return at(x_=shift(x, off, xs), core_=lax.rem(core + flip, CORES))

        loads = []
        for c in range(CHUNKS):
            copy = pltpu.make_async_copy(
                v_hbm.at[:, pl.ds(c * ROWS, ROWS), :], buf_a.at[c], load_sem.at[c]
            )
            copy.start()
            loads.append(copy)
        pot_load = pltpu.make_async_copy(pot_hbm, pot, load_sem.at[2])
        pot_load.start()
        sten_load = pltpu.make_async_copy(sten_hbm, sten, load_sem.at[3])
        sten_load.start()

        barrier = pltpu.get_barrier_semaphore()
        depth = zls * zhs
        z = zh * zls + zl
        z_up, z_down = shift(z, 1, depth), shift(z, -1, depth)
        above = at(zl_=lax.rem(z_up, zls), zh_=z_up // zls)
        below = at(zl_=lax.rem(z_down, zls), zh_=z_down // zls)
        peers = [left, right, above, below]
        peers += [at(y_=shift(y, o, ys)) for o in range(1, ys)]
        peers += [x_peer(o, c) for o, c in x_peers]
        for peer in peers:
            pl.semaphore_signal(barrier, inc=1, device_id=peer, device_id_type=pl.DeviceIdType.MESH)

        def give_tokens():
            for sem, device in ((token_up, above), (token_down, below)):
                pl.semaphore_signal(sem, inc=1, device_id=device, device_id_type=pl.DeviceIdType.MESH)

        def token_round(index):
            pl.semaphore_wait(token_up, 1)
            pl.semaphore_wait(token_down, 1)
            if index < ROUNDS - 1:
                give_tokens()

        bufs = [buf_a, buf_b]

        def split_store(s, c, plane, lanes, value):
            high = value.astype(jnp.bfloat16)
            low = (value - high.astype(jnp.float32)).astype(jnp.bfloat16)
            sbuf[s, c, HIGH_AT[plane], :, lanes] = high
            sbuf[s, c, LOW_AT[plane], :, lanes] = low

        def local_part(s, c):
            cur, nxt = bufs[s % 2], bufs[(s + 1) % 2]
            scale = (1.0 if s == 0 else 2.0) / HALF_WIDTH
            couple = [scale * KINETIC * k for k in COEFFS]
            lhs = sbuf[s, c].reshape(12 * ROWS, CELLS)
            for half in range(2):
                wide = pl.ds(half * 256, 256)
                res = jnp.dot(lhs, sten[:, wide], preferred_element_type=jnp.float32)
                res = res.reshape(12, ROWS, 256)
                for part in range(2):
                    lanes = pl.ds(half * 256 + part * LANES, LANES)
                    own = [cur[c, p, :, lanes] for p in range(PLANES)]
                    for p in range(PLANES):
                        flat = (res[HIGH_AT[p]] + res[LOW_AT[p]])[:, part * LANES : (part + 1) * LANES]
                        total = couple[1] * flat + (scale * diag[pl.ds(p, 1), lanes]) * own[p]
                        for k in range(1, PLANES):
                            if p - k >= 0 and p + k < PLANES:
                                total += couple[k] * (own[p - k] + own[p + k])
                            elif p - k >= 0:
                                total += couple[k] * own[p - k]
                            elif p + k < PLANES:
                                total += couple[k] * own[p + k]
                        if s > 0:
                            total -= nxt[c, p, :, lanes]
                        nxt[c, p, :, lanes] = total

        def finish(s, c, lanes):
            nxt = bufs[(s + 1) % 2]
            scale = (1.0 if s == 0 else 2.0) / HALF_WIDTH
            couple = [scale * KINETIC * k for k in COEFFS]
            lower = [from_left[s, c, i, :, lanes].astype(jnp.float32) for i in range(7)]
            lower[5] = lower[5] + lower[6]
            upper = [from_right[s, c, i, :, lanes].astype(jnp.float32) for i in range(7)]
            upper = [upper[1] + upper[0]] + upper[2:]
            results = []
            for p in range(PLANES):
                total = nxt[c, p, :, lanes]
                for i in range(p, PLANES):
                    total += couple[p + 6 - i] * lower[i]
                for i in range(p + 1):
                    total += couple[6 + i - p] * upper[i]
                nxt[c, p, :, lanes] = total
                results.append(total)
            return results

        halos = {}

        def send_halo(s, c, h):
            lanes = pl.ds(h * PIECE, PIECE)
            halos[s, c, h] = [
                send(
                    sbuf.at[s, c, pl.ds(start, 7), :, lanes], into.at[s, c, :, :, lanes],
                    halo_send.at[s, c, h, side], halo_recv.at[s, c, h, side], device,
                )
                for side, (start, into, device) in enumerate(((0, from_right, left), (1, from_left, right)))
            ]

        for c in range(CHUNKS):
            loads[c].wait()
            for q in range(CELLS // LANES):
                lanes = pl.ds(q * LANES, LANES)
                for p in range(PLANES):
                    split_store(0, c, p, lanes, buf_a[c, p, :, lanes])
        pl.semaphore_wait(barrier, len(peers))
        for c in range(CHUNKS):
            for h in range(PIECES):
                send_halo(0, c, h)
        give_tokens()
        pot_load.wait()
        diag[...] = pot[...] + (3.0 * KINETIC * COEFFS[0] - CENTER)
        sten_load.wait()
        for c in range(CHUNKS):
            local_part(0, c)

        zh_up, zh_down, zh_far = shift(zh, 1, zhs), shift(zh, -1, zhs), shift(zh, 2, zhs)
        sends = []
        stores = []
        arrivals = {}
        relays = {}
        y_arrivals = []

        def spread_y(c, rel, source):
            for o in range(1, ys):
                copy = send(
                    gathered.at[y, source, c], gathered.at[y, source, c],
                    y_send.at[c, rel, o - 1], y_recv.at[c, rel, o - 1], at(y_=shift(y, o, ys)),
                )
                sends.append(copy)
                y_arrivals.append(copy)

        rounds = 0
        for s in range(4):
            last = s == 3
            for c in range(CHUNKS):
                for h in range(PIECES):
                    for copy in halos[s, c, h]:
                        copy.wait_recv()
                    for q in range(h * PIECE // LANES, (h + 1) * PIECE // LANES):
                        lanes = pl.ds(q * LANES, LANES)
                        results = finish(s, c, lanes)
                        for p, value in enumerate(results):
                            if last:
                                rounded[c, q, p // 2, :, pl.ds((p % 2) * LANES, LANES)] = value.astype(jnp.bfloat16)
                            else:
                                split_store(s + 1, c, p, lanes, value)
                    if not last:
                        send_halo(s + 1, c, h)
                    if rounds < ROUNDS and (h == PIECES - 1 or (s, c) == (0, 0)):
                        token_round(rounds)
                        rounds += 1
                if not last:
                    local_part(s + 1, c)
                    continue
                first, other = (zh_up, zh_down) if c == 0 else (zh_down, zh_up)
                relays[c] = send(rounded.at[c, zh_far], relay.at[c], z_send.at[c, 2], relay_recv.at[c], at(zh_=first))
                arrivals[c, 0] = send(rounded.at[c, first], gathered.at[y, zh, c], z_send.at[c, 0], z_recv.at[c, 0], at(zh_=first))
                arrivals[c, 1] = send(rounded.at[c, other], gathered.at[y, zh, c], z_send.at[c, 1], z_recv.at[c, 1], at(zh_=other))
                gathered[y, zh, c] = rounded[c, zh]
                spread_y(c, 0, zh)
                copy = pltpu.make_async_copy(
                    buf_a.at[c], out_hbm.at[:, pl.ds(c * ROWS, ROWS), :], store_sem.at[c]
                )
                copy.start()
                stores.append(copy)

        for c in range(CHUNKS):
            first, other = (zh_up, zh_down) if c == 0 else (zh_down, zh_up)
            relays[c].wait_recv()
            arrivals[c, 2] = send(relay.at[c], gathered.at[y, other, c], relay_send.at[c], z_recv.at[c, 2], at(zh_=first))
            arrivals[c, 0].wait_recv()
            spread_y(c, 1, other)
            arrivals[c, 1].wait_recv()
            spread_y(c, 2, first)
        for c in range(CHUNKS):
            arrivals[c, 2].wait_recv()
            spread_y(c, 3, zh_far)
        for copy in y_arrivals:
            copy.wait_recv()

        own_rows = zhs * CHUNKS * ROWS
        x_arrivals = []
        for off in (2, 1, 3, 0):
            dest = shift(x, off, xs)
            total = jnp.zeros((own_rows, own_rows), jnp.float32)
            for i in range(PLANES // 2):
                total += lax.dot_general(
                    gathered[dest, :, :, i].reshape(own_rows, 2 * LANES),
                    gathered[y, :, :, i].reshape(own_rows, 2 * LANES),
                    (((1,), (1,)), ((), ())),
                    preferred_element_type=jnp.float32,
                )
            total = total.reshape(zls, CORES, 8, own_rows)
            for b in range(CORES):
                parts[off, b] = total[:, b]
            for flip in range(CORES):
                if (off, flip) == (0, 0):
                    continue
                copy = send(
                    parts.at[off, lax.rem(core + flip, CORES)], got_x.at[off, flip],
                    x_send.at[off, flip], x_recv.at[off, flip], x_peer(off, flip),
                )
                sends.append(copy)
                x_arrivals.append((off, flip, copy))
        total = parts[0, core]
        for off, flip, copy in x_arrivals:
            copy.wait_recv()
            total += got_x[off, flip]
        sum_x[...] = total

        zl_arrivals = []
        for o in range(1, zls):
            dest = shift(zl, o, zls)
            copy = send(sum_x.at[dest], got_zl.at[o], zl_send.at[o], zl_recv.at[o], at(zl_=dest))
            sends.append(copy)
            zl_arrivals.append(copy)
        total = sum_x[zl]
        for o, copy in enumerate(zl_arrivals):
            copy.wait_recv()
            total += got_zl[o + 1]
        sum_zl[...] = total

        zh_arrivals = []
        for o in range(1, zhs):
            dest = shift(zh, o, zhs)
            copy = send(sum_zl, got_zh.at[o], zh_send.at[o], zh_recv.at[o], at(zh_=dest))
            sends.append(copy)
            zh_arrivals.append(copy)
        for o, copy in enumerate(zh_arrivals):
            copy.wait_recv()
            total += got_zh[o + 1]
        width = CHUNKS * ROWS
        mine = jnp.zeros((8, width), jnp.float32)
        for o in range(zhs):
            mine = jnp.where(zh == o, total[:, o * width : (o + 1) * width], mine)
        corr_ref[...] = mine * (1.0 / (NZ * CELLS))

        for copy in [one for pair in halos.values() for one in pair]:
            copy.wait_send()
        for copy in list(relays.values()) + list(arrivals.values()) + sends:
            copy.wait_send()
        for copy in stores:
            copy.wait()

    return kernel


def solution(mesh):
    zls, zhs = 8, 4
    xs = mesh.shape["dom"] // (zls * CORES)
    ys = mesh.shape["grp"] // zhs
    stencil = plane_stencil()

    def shards(orbitals, potential):
        planes = jnp.transpose(orbitals, (1, 0, 2))
        count = planes.shape[1]
        dma = pltpu.SemaphoreType.DMA
        f32, bf16 = jnp.float32, jnp.bfloat16
        filtered, corr = pl.pallas_call(
            make_kernel(xs, zls, ys, zhs),
            out_shape=(
                jax.ShapeDtypeStruct((PLANES, count, CELLS), f32),
                jax.ShapeDtypeStruct((8, count), f32),
            ),
            in_specs=[pl.BlockSpec(memory_space=pl.ANY)] * 3,
            out_specs=(
                pl.BlockSpec(memory_space=pl.ANY),
                pl.BlockSpec(memory_space=pltpu.VMEM),
            ),
            scratch_shapes=[
                pltpu.VMEM((CHUNKS, PLANES, ROWS, CELLS), f32),
                pltpu.VMEM((CHUNKS, PLANES, ROWS, CELLS), f32),
                pltpu.VMEM((CELLS, CELLS), bf16),
                pltpu.VMEM((PLANES, CELLS), f32),
                pltpu.VMEM((PLANES, CELLS), f32),
                pltpu.VMEM((4, CHUNKS, 12, ROWS, CELLS), bf16),
                pltpu.VMEM((4, CHUNKS, 7, ROWS, CELLS), bf16),
                pltpu.VMEM((4, CHUNKS, 7, ROWS, CELLS), bf16),
                pltpu.VMEM((CHUNKS, zhs, 3, ROWS, 2 * LANES), bf16),
                pltpu.VMEM((CHUNKS, 3, ROWS, 2 * LANES), bf16),
                pltpu.VMEM((ys, zhs, CHUNKS, 3, ROWS, 2 * LANES), bf16),
                pltpu.VMEM((xs, CORES, zls, 8, LANES), f32),
                pltpu.VMEM((xs, CORES, zls, 8, LANES), f32),
                pltpu.VMEM((zls, 8, LANES), f32),
                pltpu.VMEM((zls, 8, LANES), f32),
                pltpu.VMEM((8, LANES), f32),
                pltpu.VMEM((zhs, 8, LANES), f32),
                dma((4,)),
                dma((CHUNKS,)),
                pltpu.SemaphoreType.REGULAR,
                pltpu.SemaphoreType.REGULAR,
                dma((4, CHUNKS, PIECES, 2)),
                dma((4, CHUNKS, PIECES, 2)),
                dma((CHUNKS, 3)),
                dma((CHUNKS, 3)),
                dma((CHUNKS,)),
                dma((CHUNKS,)),
                dma((CHUNKS, 4, 3)),
                dma((CHUNKS, 4, 3)),
                dma((xs, CORES)),
                dma((xs, CORES)),
                dma((zls,)),
                dma((zls,)),
                dma((zhs,)),
                dma((zhs,)),
            ],
            compiler_params=pltpu.CompilerParams(
                collective_id=0, has_side_effects=True, vmem_limit_bytes=60 * 1024 * 1024
            ),
            cost_estimate=pl.CostEstimate(flops=10**9, bytes_accessed=1500000, transcendentals=0),
        )(planes, potential, jnp.asarray(stencil))
        return jnp.transpose(filtered, (1, 0, 2)), jnp.transpose(corr, (1, 0))

    in_specs = (P("grp", "dom", None), P("dom", None))
    out_specs = (P("grp", "dom", None), P("grp", "dom"))
    return jax.shard_map(shards, mesh=mesh, in_specs=in_specs, out_specs=out_specs, check_vma=False)
```

```python
import jax
import jax.numpy as jnp
import ml_dtypes
import numpy as np
from jax import lax
from jax.experimental import pallas as pl
from jax.experimental.pallas import tpu as pltpu
from jax.sharding import PartitionSpec as P

NX = 32
NY = 16
CELLS = NX * NY
NZ = 384
CORES = 2
CHUNKS = 2
ROWS = 16
LANES = 128
PLANES = 6
PIECES = 2
PIECE = CELLS // PIECES
ROUNDS = 7
RELAY = True

COEFFS = [
    -5369.0 / 1800.0,
    12.0 / 7.0,
    -15.0 / 56.0,
    10.0 / 189.0,
    -1.0 / 112.0,
    2.0 / 1925.0,
    -1.0 / 16632.0,
]
CENTER = 13.0
HALF_WIDTH = 11.0
KINETIC = -0.5 / 0.25

HIGH_AT = [1, 2, 3, 4, 5, 6]
LOW_AT = [0, 8, 9, 10, 11, 7]


def plane_stencil():
    cells = np.arange(CELLS)
    row_of, col_of = cells // NX, cells % NX
    row_gap = (row_of[:, None] - row_of[None, :]) % NY
    col_gap = (col_of[:, None] - col_of[None, :]) % NX
    stencil = np.zeros((CELLS, CELLS), np.float64)
    for reach in range(1, 7):
        rows = (col_gap == 0) & ((row_gap == reach) | (row_gap == NY - reach))
        cols = (row_gap == 0) & ((col_gap == reach) | (col_gap == NX - reach))
        stencil += COEFFS[reach] / COEFFS[1] * (rows.astype(np.float64) + cols.astype(np.float64))
    return stencil.astype(ml_dtypes.bfloat16)


def make_kernel(xs, zls, ys, zhs):
    doms = xs * zls * CORES

    def kernel(
        v_hbm, pot_hbm, sten_hbm, out_hbm, corr_ref,
        buf_a, buf_b, sten, pot, diag, sbuf, from_left, from_right,
        rounded, relay, gathered, parts, got_x, packed, got_z,
        load_sem, store_sem, token_up, token_down, halo_send, halo_recv, z_send, z_recv, relay_recv, relay_send,
        y_send, y_recv, x_send, x_recv, d_send, d_recv,
    ):
        dom = lax.axis_index("dom")
        grp = lax.axis_index("grp")
        core = lax.rem(dom, CORES)
        zl = lax.rem(dom // CORES, zls)
        x = dom // (CORES * zls)
        zh = lax.rem(grp, zhs)
        y = grp // zhs

        def at(x_=x, zl_=zl, core_=core, y_=y, zh_=zh):
            return {"dom": (x_ * zls + zl_) * CORES + core_, "grp": y_ * zhs + zh_}

        def shift(value, by, count):
            return lax.rem(value + (by + count), count)

        def send(src, dst, send_sem, recv_sem, device):
            copy = pltpu.make_async_remote_copy(
                src_ref=src, dst_ref=dst, send_sem=send_sem, recv_sem=recv_sem,
                device_id=device, device_id_type=pl.DeviceIdType.MESH,
            )
            copy.start()
            return copy

        left = {"dom": shift(dom, -1, doms), "grp": grp}
        right = {"dom": shift(dom, 1, doms), "grp": grp}
        x_peers = [(o, c) for o in range(xs) for c in range(CORES) if (o, c) != (0, 0)]

        def x_peer(off, flip):
            return at(x_=shift(x, off, xs), core_=lax.rem(core + flip, CORES))

        loads = []
        for c in range(CHUNKS):
            copy = pltpu.make_async_copy(
                v_hbm.at[:, pl.ds(c * ROWS, ROWS), :], buf_a.at[c], load_sem.at[c]
            )
            copy.start()
            loads.append(copy)
        pot_load = pltpu.make_async_copy(pot_hbm, pot, load_sem.at[2])
        pot_load.start()
        sten_load = pltpu.make_async_copy(sten_hbm, sten, load_sem.at[3])
        sten_load.start()

        barrier = pltpu.get_barrier_semaphore()
        depth = zls * zhs
        z = zh * zls + zl
        z_up, z_down = shift(z, 1, depth), shift(z, -1, depth)
        above = at(zl_=lax.rem(z_up, zls), zh_=z_up // zls)
        below = at(zl_=lax.rem(z_down, zls), zh_=z_down // zls)
        peers = [left, right, above, below]
        peers += [at(y_=shift(y, o, ys)) for o in range(1, ys)]
        peers += [x_peer(o, c) for o, c in x_peers]
        for peer in peers:
            pl.semaphore_signal(barrier, inc=1, device_id=peer, device_id_type=pl.DeviceIdType.MESH)

        def give_tokens():
            for sem, device in ((token_up, above), (token_down, below)):
                pl.semaphore_signal(sem, inc=1, device_id=device, device_id_type=pl.DeviceIdType.MESH)

        def token_round(index):
            pl.semaphore_wait(token_up, 1)
            pl.semaphore_wait(token_down, 1)
            if index < ROUNDS - 1:
                give_tokens()

        bufs = [buf_a, buf_b]

        def split_store(s, c, plane, lanes, value):
            high = value.astype(jnp.bfloat16)
            low = (value - high.astype(jnp.float32)).astype(jnp.bfloat16)
            sbuf[s, c, HIGH_AT[plane], :, lanes] = high
            sbuf[s, c, LOW_AT[plane], :, lanes] = low

        def local_part(s, c):
            cur, nxt = bufs[s % 2], bufs[(s + 1) % 2]
            scale = (1.0 if s == 0 else 2.0) / HALF_WIDTH
            couple = [scale * KINETIC * k for k in COEFFS]
            lhs = sbuf[s, c].reshape(12 * ROWS, CELLS)
            for half in range(2):
                wide = pl.ds(half * 256, 256)
                res = jnp.dot(lhs, sten[:, wide], preferred_element_type=jnp.float32)
                res = res.reshape(12, ROWS, 256)
                for part in range(2):
                    lanes = pl.ds(half * 256 + part * LANES, LANES)
                    own = [cur[c, p, :, lanes] for p in range(PLANES)]
                    for p in range(PLANES):
                        flat = (res[HIGH_AT[p]] + res[LOW_AT[p]])[:, part * LANES : (part + 1) * LANES]
                        total = couple[1] * flat + (scale * diag[pl.ds(p, 1), lanes]) * own[p]
                        for k in range(1, PLANES):
                            if p - k >= 0 and p + k < PLANES:
                                total += couple[k] * (own[p - k] + own[p + k])
                            elif p - k >= 0:
                                total += couple[k] * own[p - k]
                            elif p + k < PLANES:
                                total += couple[k] * own[p + k]
                        if s > 0:
                            total -= nxt[c, p, :, lanes]
                        nxt[c, p, :, lanes] = total

        def finish(s, c, lanes):
            nxt = bufs[(s + 1) % 2]
            scale = (1.0 if s == 0 else 2.0) / HALF_WIDTH
            couple = [scale * KINETIC * k for k in COEFFS]
            lower = [from_left[s, c, i, :, lanes].astype(jnp.float32) for i in range(7)]
            lower[5] = lower[5] + lower[6]
            upper = [from_right[s, c, i, :, lanes].astype(jnp.float32) for i in range(7)]
            upper = [upper[1] + upper[0]] + upper[2:]
            results = []
            for p in range(PLANES):
                total = nxt[c, p, :, lanes]
                for i in range(p, PLANES):
                    total += couple[p + 6 - i] * lower[i]
                for i in range(p + 1):
                    total += couple[6 + i - p] * upper[i]
                nxt[c, p, :, lanes] = total * 0.5 if s == 3 else total
                results.append(total)
            return results

        halos = {}

        def send_halo(s, c, h):
            lanes = pl.ds(h * PIECE, PIECE)
            halos[s, c, h] = [
                send(
                    sbuf.at[s, c, pl.ds(start, 7), :, lanes], into.at[s, c, :, :, lanes],
                    halo_send.at[s, c, h, side], halo_recv.at[s, c, h, side], device,
                )
                for side, (start, into, device) in enumerate(((0, from_right, left), (1, from_left, right)))
            ]

        for c in range(CHUNKS):
            loads[c].wait()
            for q in range(CELLS // LANES):
                lanes = pl.ds(q * LANES, LANES)
                for p in range(PLANES):
                    split_store(0, c, p, lanes, buf_a[c, p, :, lanes])
        pl.semaphore_wait(barrier, len(peers))
        for c in range(CHUNKS):
            for h in range(PIECES):
                send_halo(0, c, h)
        give_tokens()
        pot_load.wait()
        diag[...] = pot[...] + (3.0 * KINETIC * COEFFS[0] - CENTER)
        sten_load.wait()
        for c in range(CHUNKS):
            local_part(0, c)

        zh_up, zh_down, zh_far = shift(zh, 1, zhs), shift(zh, -1, zhs), shift(zh, 2, zhs)
        sends = []
        stores = []
        arrivals = {}
        relays = {}
        y_arrivals = []

        def spread_y(c, rel, source):
            for o in range(1, ys):
                copy = send(
                    gathered.at[y, source, c], gathered.at[y, source, c],
                    y_send.at[c, rel, o - 1], y_recv.at[c, rel, o - 1], at(y_=shift(y, o, ys)),
                )
                sends.append(copy)
                y_arrivals.append(copy)

        rounds = 0
        for s in range(4):
            last = s == 3
            for c in range(CHUNKS):
                for h in range(PIECES):
                    for copy in halos[s, c, h]:
                        copy.wait_recv()
                    for q in range(h * PIECE // LANES, (h + 1) * PIECE // LANES):
                        lanes = pl.ds(q * LANES, LANES)
                        results = finish(s, c, lanes)
                        for p, value in enumerate(results):
                            if last:
                                rounded[c, q, p // 2, :, pl.ds((p % 2) * LANES, LANES)] = value.astype(jnp.bfloat16)
                            else:
                                split_store(s + 1, c, p, lanes, value)
                    if not last:
                        send_halo(s + 1, c, h)
                    if rounds < ROUNDS and (h == PIECES - 1 or (s, c) == (0, 0)):
                        token_round(rounds)
                        rounds += 1
                if not last:
                    local_part(s + 1, c)
                    continue
                first, other = (zh_up, zh_down) if c == 0 else (zh_down, zh_up)
                if RELAY:
                    relays[c] = send(rounded.at[c, zh_far], relay.at[c], z_send.at[c, 2], relay_recv.at[c], at(zh_=first))
                else:
                    arrivals[c, 2] = send(rounded.at[c, zh_far], gathered.at[y, zh, c], z_send.at[c, 2], z_recv.at[c, 2], at(zh_=zh_far))
                arrivals[c, 0] = send(rounded.at[c, first], gathered.at[y, zh, c], z_send.at[c, 0], z_recv.at[c, 0], at(zh_=first))
                arrivals[c, 1] = send(rounded.at[c, other], gathered.at[y, zh, c], z_send.at[c, 1], z_recv.at[c, 1], at(zh_=other))
                gathered[y, zh, c] = rounded[c, zh]
                spread_y(c, 0, zh)
                copy = pltpu.make_async_copy(
                    buf_a.at[c], out_hbm.at[:, pl.ds(c * ROWS, ROWS), :], store_sem.at[c]
                )
                copy.start()
                stores.append(copy)

        for c in range(CHUNKS):
            first, other = (zh_up, zh_down) if c == 0 else (zh_down, zh_up)
            if RELAY:
                relays[c].wait_recv()
                arrivals[c, 2] = send(relay.at[c], gathered.at[y, other, c], relay_send.at[c], z_recv.at[c, 2], at(zh_=first))
        for c in range(CHUNKS):
            first, other = (zh_up, zh_down) if c == 0 else (zh_down, zh_up)
            arrivals[c, 0].wait_recv()
            spread_y(c, 1, other)
            arrivals[c, 1].wait_recv()
            spread_y(c, 2, first)
        for c in range(CHUNKS):
            arrivals[c, 2].wait_recv()
            spread_y(c, 3, zh_far)
        for copy in y_arrivals:
            copy.wait_recv()

        own_rows = zhs * CHUNKS * ROWS
        x_arrivals = []
        for off in (2, 1, 3, 0):
            dest = shift(x, off, xs)
            total = jnp.zeros((own_rows, own_rows), jnp.float32)
            for i in range(PLANES // 2):
                total += lax.dot_general(
                    gathered[dest, :, :, i].reshape(own_rows, 2 * LANES),
                    gathered[y, :, :, i].reshape(own_rows, 2 * LANES),
                    (((1,), (1,)), ((), ())),
                    preferred_element_type=jnp.float32,
                )
            total = total.reshape(zls, CORES, 8, own_rows)
            for b in range(CORES):
                parts[off, b] = total[:, b].reshape(zls // 2, 16, own_rows).astype(jnp.bfloat16)
            for flip in range(CORES):
                if (off, flip) == (0, 0):
                    continue
                copy = send(
                    parts.at[off, lax.rem(core + flip, CORES)], got_x.at[off, flip],
                    x_send.at[off, flip], x_recv.at[off, flip], x_peer(off, flip),
                )
                sends.append(copy)
                x_arrivals.append((off, flip, copy))
        total = parts[0, core].astype(jnp.float32)
        for off, flip, copy in x_arrivals:
            copy.wait_recv()
            total += got_x[off, flip].astype(jnp.float32)
        total = total.reshape(zls, 8, LANES)

        width = CHUNKS * ROWS
        row = lax.broadcasted_iota(jnp.int32, (8, LANES), 0) % 4
        block = lax.broadcasted_iota(jnp.int32, (8, LANES), 1) // width
        for l in range(zls):
            turned = [total[l]] + [pltpu.roll(total[l], k * width, 1) for k in range(1, 4)]
            for h in range(zhs):
                mixed = jnp.zeros((8, LANES), jnp.float32)
                for b in range(4):
                    mixed = jnp.where((row == b) & (block == b), turned[(b - h) % 4], mixed)
                mixed = mixed + pltpu.roll(mixed, 7, 0)
                mixed = mixed + pltpu.roll(mixed, 6, 0)
                packed[h * zls + l, pl.ds(0, 1)] = mixed[0:1]
                packed[h * zls + l, pl.ds(1, 1)] = mixed[4:5]
        d_arrivals = []
        for o in sorted(range(1, depth), key=lambda o: -min(o, depth - o)):
            dest = shift(z, o, depth)
            copy = send(
                packed.at[dest], got_z.at[o], d_send.at[o], d_recv.at[o],
                at(zl_=lax.rem(dest, zls), zh_=dest // zls),
            )
            sends.append(copy)
            d_arrivals.append((o, copy))
        total = packed[z]
        for o, copy in reversed(d_arrivals):
            copy.wait_recv()
            total += got_z[o]
        for a in range(2):
            for b in range(4):
                corr_ref[pl.ds(4 * a + b, 1), :] = total[a : a + 1, b * width : (b + 1) * width]

        for copy in [one for pair in halos.values() for one in pair]:
            copy.wait_send()
        for copy in list(relays.values()) + list(arrivals.values()) + sends:
            copy.wait_send()
        for copy in stores:
            copy.wait()

    return kernel


def solution(mesh):
    zls, zhs = 8, 4
    xs = mesh.shape["dom"] // (zls * CORES)
    ys = mesh.shape["grp"] // zhs
    stencil = plane_stencil()

    def shards(orbitals, potential):
        planes = jnp.transpose(orbitals, (1, 0, 2))
        count = planes.shape[1]
        dma = pltpu.SemaphoreType.DMA
        f32, bf16 = jnp.float32, jnp.bfloat16
        filtered, corr = pl.pallas_call(
            make_kernel(xs, zls, ys, zhs),
            out_shape=(
                jax.ShapeDtypeStruct((PLANES, count, CELLS), f32),
                jax.ShapeDtypeStruct((8, count), f32),
            ),
            in_specs=[pl.BlockSpec(memory_space=pl.ANY)] * 3,
            out_specs=(
                pl.BlockSpec(memory_space=pl.ANY),
                pl.BlockSpec(memory_space=pltpu.VMEM),
            ),
            scratch_shapes=[
                pltpu.VMEM((CHUNKS, PLANES, ROWS, CELLS), f32),
                pltpu.VMEM((CHUNKS, PLANES, ROWS, CELLS), f32),
                pltpu.VMEM((CELLS, CELLS), bf16),
                pltpu.VMEM((PLANES, CELLS), f32),
                pltpu.VMEM((PLANES, CELLS), f32),
                pltpu.VMEM((4, CHUNKS, 12, ROWS, CELLS), bf16),
                pltpu.VMEM((4, CHUNKS, 7, ROWS, CELLS), bf16),
                pltpu.VMEM((4, CHUNKS, 7, ROWS, CELLS), bf16),
                pltpu.VMEM((CHUNKS, zhs, 3, ROWS, 2 * LANES), bf16),
                pltpu.VMEM((CHUNKS, 3, ROWS, 2 * LANES), bf16),
                pltpu.VMEM((ys, zhs, CHUNKS, 3, ROWS, 2 * LANES), bf16),
                pltpu.VMEM((xs, CORES, zls // 2, 16, LANES), bf16),
                pltpu.VMEM((xs, CORES, zls // 2, 16, LANES), bf16),
                pltpu.VMEM((zls * zhs, 2, LANES), f32),
                pltpu.VMEM((zls * zhs, 2, LANES), f32),
                dma((4,)),
                dma((CHUNKS,)),
                pltpu.SemaphoreType.REGULAR,
                pltpu.SemaphoreType.REGULAR,
                dma((4, CHUNKS, PIECES, 2)),
                dma((4, CHUNKS, PIECES, 2)),
                dma((CHUNKS, 3)),
                dma((CHUNKS, 3)),
                dma((CHUNKS,)),
                dma((CHUNKS,)),
                dma((CHUNKS, 4, 3)),
                dma((CHUNKS, 4, 3)),
                dma((xs, CORES)),
                dma((xs, CORES)),
                dma((zls * zhs,)),
                dma((zls * zhs,)),
            ],
            compiler_params=pltpu.CompilerParams(
                collective_id=0, has_side_effects=True, vmem_limit_bytes=60 * 1024 * 1024
            ),
            cost_estimate=pl.CostEstimate(flops=10**9, bytes_accessed=1500000, transcendentals=0),
        )(planes, potential, jnp.asarray(stencil))
        return jnp.transpose(2.0 * filtered, (1, 0, 2)), jnp.transpose(corr, (1, 0)) * (1.0 / (NZ * CELLS))

    in_specs = (P("grp", "dom", None), P("dom", None))
    out_specs = (P("grp", "dom", None), P("grp", "dom"))
    return jax.shard_map(shards, mesh=mesh, in_specs=in_specs, out_specs=out_specs, check_vma=False)
```

```python
import jax
import jax.numpy as jnp
import ml_dtypes
import numpy as np
from jax import lax
from jax.experimental import pallas as pl
from jax.experimental.pallas import tpu as pltpu
from jax.sharding import PartitionSpec as P

NX = 32
NY = 16
CELLS = NX * NY
NZ = 384
CORES = 2
CHUNKS = 2
ROWS = 16
LANES = 128
PLANES = 6
PIECES = 2
PIECE = CELLS // PIECES
ROUNDS = 7

COEFFS = [
    -5369.0 / 1800.0,
    12.0 / 7.0,
    -15.0 / 56.0,
    10.0 / 189.0,
    -1.0 / 112.0,
    2.0 / 1925.0,
    -1.0 / 16632.0,
]
CENTER = 13.0
HALF_WIDTH = 11.0
KINETIC = -0.5 / 0.25

HIGH_AT = [1, 2, 3, 4, 5, 6]
LOW_AT = [0, 8, 9, 10, 11, 7]


def plane_stencil():
    cells = np.arange(CELLS)
    row_of, col_of = cells // NX, cells % NX
    row_gap = (row_of[:, None] - row_of[None, :]) % NY
    col_gap = (col_of[:, None] - col_of[None, :]) % NX
    stencil = np.zeros((CELLS, CELLS), np.float64)
    for reach in range(1, 7):
        rows = (col_gap == 0) & ((row_gap == reach) | (row_gap == NY - reach))
        cols = (row_gap == 0) & ((col_gap == reach) | (col_gap == NX - reach))
        stencil += COEFFS[reach] / COEFFS[1] * (rows.astype(np.float64) + cols.astype(np.float64))
    return stencil.astype(ml_dtypes.bfloat16)


def make_kernel(xs, zls, ys, zhs):
    doms = xs * zls * CORES

    def kernel(
        v_hbm, pot_hbm, sten_hbm, out_hbm, corr_ref,
        buf_a, buf_b, sten, pot, diag, sbuf, from_left, from_right,
        rounded, relay, gathered, parts, got_x, packed, got_z,
        load_sem, store_sem, token_up, token_down, halo_send, halo_recv, z_send, z_recv, relay_recv, relay_send,
        y_send, y_recv, x_send, x_recv, d_send, d_recv,
    ):
        dom = lax.axis_index("dom")
        grp = lax.axis_index("grp")
        core = lax.rem(dom, CORES)
        zl = lax.rem(dom // CORES, zls)
        x = dom // (CORES * zls)
        zh = lax.rem(grp, zhs)
        y = grp // zhs

        def at(x_=x, zl_=zl, core_=core, y_=y, zh_=zh):
            return {"dom": (x_ * zls + zl_) * CORES + core_, "grp": y_ * zhs + zh_}

        def shift(value, by, count):
            return lax.rem(value + (by + count), count)

        def send(src, dst, send_sem, recv_sem, device):
            copy = pltpu.make_async_remote_copy(
                src_ref=src, dst_ref=dst, send_sem=send_sem, recv_sem=recv_sem,
                device_id=device, device_id_type=pl.DeviceIdType.MESH,
            )
            copy.start()
            return copy

        left = {"dom": shift(dom, -1, doms), "grp": grp}
        right = {"dom": shift(dom, 1, doms), "grp": grp}
        x_peers = [(o, c) for o in range(xs) for c in range(CORES) if (o, c) != (0, 0)]

        def x_peer(off, flip):
            return at(x_=shift(x, off, xs), core_=lax.rem(core + flip, CORES))

        loads = []
        for c in range(CHUNKS):
            copy = pltpu.make_async_copy(
                v_hbm.at[:, pl.ds(c * ROWS, ROWS), :], buf_a.at[c], load_sem.at[c]
            )
            copy.start()
            loads.append(copy)
        pot_load = pltpu.make_async_copy(pot_hbm, pot, load_sem.at[2])
        pot_load.start()
        sten_load = pltpu.make_async_copy(sten_hbm, sten, load_sem.at[3])
        sten_load.start()

        barrier = pltpu.get_barrier_semaphore()
        depth = zls * zhs
        z = zh * zls + zl
        z_up, z_down = shift(z, 1, depth), shift(z, -1, depth)
        above = at(zl_=lax.rem(z_up, zls), zh_=z_up // zls)
        below = at(zl_=lax.rem(z_down, zls), zh_=z_down // zls)
        peers = [left, right, above, below]
        peers += [at(y_=shift(y, o, ys)) for o in range(1, ys)]
        peers += [x_peer(o, c) for o, c in x_peers]
        for peer in peers:
            pl.semaphore_signal(barrier, inc=1, device_id=peer, device_id_type=pl.DeviceIdType.MESH)

        def give_tokens():
            for sem, device in ((token_up, above), (token_down, below)):
                pl.semaphore_signal(sem, inc=1, device_id=device, device_id_type=pl.DeviceIdType.MESH)

        def token_round(index):
            pl.semaphore_wait(token_up, 1)
            pl.semaphore_wait(token_down, 1)
            if index < ROUNDS - 1:
                give_tokens()

        bufs = [buf_a, buf_b]

        def split_store(s, c, plane, lanes, value):
            high = value.astype(jnp.bfloat16)
            low = (value - high.astype(jnp.float32)).astype(jnp.bfloat16)
            sbuf[s, c, HIGH_AT[plane], :, lanes] = high
            sbuf[s, c, LOW_AT[plane], :, lanes] = low

        def local_part(s, c):
            cur, nxt = bufs[s % 2], bufs[(s + 1) % 2]
            scale = (1.0 if s == 0 else 2.0) / HALF_WIDTH
            couple = [scale * KINETIC * k for k in COEFFS]
            lhs = sbuf[s, c].reshape(12 * ROWS, CELLS)
            for half in range(2):
                wide = pl.ds(half * 256, 256)
                res = jnp.dot(lhs, sten[:, wide], preferred_element_type=jnp.float32)
                res = res.reshape(12, ROWS, 256)
                for part in range(2):
                    lanes = pl.ds(half * 256 + part * LANES, LANES)
                    own = [cur[c, p, :, lanes] for p in range(PLANES)]
                    for p in range(PLANES):
                        flat = (res[HIGH_AT[p]] + res[LOW_AT[p]])[:, part * LANES : (part + 1) * LANES]
                        total = couple[1] * flat + (scale * diag[pl.ds(p, 1), lanes]) * own[p]
                        for k in range(1, PLANES):
                            if p - k >= 0 and p + k < PLANES:
                                total += couple[k] * (own[p - k] + own[p + k])
                            elif p - k >= 0:
                                total += couple[k] * own[p - k]
                            elif p + k < PLANES:
                                total += couple[k] * own[p + k]
                        if s > 0:
                            total -= nxt[c, p, :, lanes]
                        nxt[c, p, :, lanes] = total

        def finish(s, c, lanes):
            nxt = bufs[(s + 1) % 2]
            scale = (1.0 if s == 0 else 2.0) / HALF_WIDTH
            couple = [scale * KINETIC * k for k in COEFFS]
            lower = [from_left[s, c, i, :, lanes].astype(jnp.float32) for i in range(7)]
            lower[5] = lower[5] + lower[6]
            upper = [from_right[s, c, i, :, lanes].astype(jnp.float32) for i in range(7)]
            upper = [upper[1] + upper[0]] + upper[2:]
            results = []
            for p in range(PLANES):
                total = nxt[c, p, :, lanes]
                for i in range(p, PLANES):
                    total += couple[p + 6 - i] * lower[i]
                for i in range(p + 1):
                    total += couple[6 + i - p] * upper[i]
                nxt[c, p, :, lanes] = total * 0.5 if s == 3 else total
                results.append(total)
            return results

        halos = {}

        def send_halo(s, c, h):
            lanes = pl.ds(h * PIECE, PIECE)
            halos[s, c, h] = [
                send(
                    sbuf.at[s, c, pl.ds(start, 7), :, lanes], into.at[s, c, :, :, lanes],
                    halo_send.at[s, c, h, side], halo_recv.at[s, c, h, side], device,
                )
                for side, (start, into, device) in enumerate(((0, from_right, left), (1, from_left, right)))
            ]

        for c in range(CHUNKS):
            loads[c].wait()
            for q in range(CELLS // LANES):
                lanes = pl.ds(q * LANES, LANES)
                for p in range(PLANES):
                    split_store(0, c, p, lanes, buf_a[c, p, :, lanes])
            if c == 0:
                pl.semaphore_wait(barrier, len(peers))
            for h in range(PIECES):
                send_halo(0, c, h)
        give_tokens()
        pot_load.wait()
        diag[...] = pot[...] + (3.0 * KINETIC * COEFFS[0] - CENTER)
        sten_load.wait()
        for c in range(CHUNKS):
            local_part(0, c)

        zh_up, zh_down, zh_far = shift(zh, 1, zhs), shift(zh, -1, zhs), shift(zh, 2, zhs)
        sends = []
        stores = []
        arrivals = {}
        relays = {}
        y_arrivals = []

        def spread_y(c, rel, source):
            for o in range(1, ys):
                copy = send(
                    gathered.at[y, source, c], gathered.at[y, source, c],
                    y_send.at[c, rel, o - 1], y_recv.at[c, rel, o - 1], at(y_=shift(y, o, ys)),
                )
                sends.append(copy)
                y_arrivals.append(copy)

        rounds = 0
        for s in range(4):
            last = s == 3
            for c in range(CHUNKS):
                for h in range(PIECES):
                    for copy in halos[s, c, h]:
                        copy.wait_recv()
                    for q in range(h * PIECE // LANES, (h + 1) * PIECE // LANES):
                        lanes = pl.ds(q * LANES, LANES)
                        results = finish(s, c, lanes)
                        for p, value in enumerate(results):
                            if last:
                                rounded[c, q, p // 2, :, pl.ds((p % 2) * LANES, LANES)] = value.astype(jnp.bfloat16)
                            else:
                                split_store(s + 1, c, p, lanes, value)
                    if not last:
                        send_halo(s + 1, c, h)
                    if rounds < ROUNDS and (h == PIECES - 1 or (s, c) == (0, 0)):
                        token_round(rounds)
                        rounds += 1
                if not last:
                    local_part(s + 1, c)
                    continue
                first, other = (zh_up, zh_down) if c == 0 else (zh_down, zh_up)
                relays[c] = send(rounded.at[c, zh_far], relay.at[c], z_send.at[c, 2], relay_recv.at[c], at(zh_=first))
                gathered[y, zh, c] = rounded[c, zh]
                spread_y(c, 0, zh)
                copy = pltpu.make_async_copy(
                    buf_a.at[c], out_hbm.at[:, pl.ds(c * ROWS, ROWS), :], store_sem.at[c]
                )
                copy.start()
                stores.append(copy)

        for c in range(CHUNKS):
            first, other = (zh_up, zh_down) if c == 0 else (zh_down, zh_up)
            relays[c].wait_send()
            arrivals[c, 0] = send(rounded.at[c, first], gathered.at[y, zh, c], z_send.at[c, 0], z_recv.at[c, 0], at(zh_=first))
            arrivals[c, 1] = send(rounded.at[c, other], gathered.at[y, zh, c], z_send.at[c, 1], z_recv.at[c, 1], at(zh_=other))
        for c in range(CHUNKS):
            first, other = (zh_up, zh_down) if c == 0 else (zh_down, zh_up)
            relays[c].wait_recv()
            arrivals[c, 2] = send(relay.at[c], gathered.at[y, other, c], relay_send.at[c], z_recv.at[c, 2], at(zh_=first))
        for c in range(CHUNKS):
            first, other = (zh_up, zh_down) if c == 0 else (zh_down, zh_up)
            arrivals[c, 0].wait_recv()
            spread_y(c, 1, other)
            arrivals[c, 1].wait_recv()
            spread_y(c, 2, first)
        for c in range(CHUNKS):
            arrivals[c, 2].wait_recv()
            spread_y(c, 3, zh_far)
        for copy in y_arrivals:
            copy.wait_recv()

        own_rows = zhs * CHUNKS * ROWS
        x_arrivals = []
        for off in (2, 1, 3, 0):
            dest = shift(x, off, xs)
            total = jnp.zeros((own_rows, own_rows), jnp.float32)
            for i in range(PLANES // 2):
                total += lax.dot_general(
                    gathered[dest, :, :, i].reshape(own_rows, 2 * LANES),
                    gathered[y, :, :, i].reshape(own_rows, 2 * LANES),
                    (((1,), (1,)), ((), ())),
                    preferred_element_type=jnp.float32,
                )
            total = total.reshape(zls, CORES, 8, own_rows)
            for b in range(CORES):
                parts[off, b] = total[:, b].reshape(zls // 2, 16, own_rows).astype(jnp.bfloat16)
            for flip in range(CORES):
                if (off, flip) == (0, 0):
                    continue
                copy = send(
                    parts.at[off, lax.rem(core + flip, CORES)], got_x.at[off, flip],
                    x_send.at[off, flip], x_recv.at[off, flip], x_peer(off, flip),
                )
                sends.append(copy)
                x_arrivals.append((off, flip, copy))
        total = parts[0, core].astype(jnp.float32)
        for off, flip, copy in x_arrivals:
            copy.wait_recv()
            total += got_x[off, flip].astype(jnp.float32)
        total = total.reshape(zls, 8, LANES)

        width = CHUNKS * ROWS
        row = lax.broadcasted_iota(jnp.int32, (8, LANES), 0) % 4
        block = lax.broadcasted_iota(jnp.int32, (8, LANES), 1) // width
        for l in range(zls):
            turned = [total[l]] + [pltpu.roll(total[l], k * width, 1) for k in range(1, 4)]
            for h in range(zhs):
                mixed = jnp.zeros((8, LANES), jnp.float32)
                for b in range(4):
                    mixed = jnp.where((row == b) & (block == b), turned[(b - h) % 4], mixed)
                mixed = mixed + pltpu.roll(mixed, 7, 0)
                mixed = mixed + pltpu.roll(mixed, 6, 0)
                packed[h * zls + l, pl.ds(0, 1)] = mixed[0:1]
                packed[h * zls + l, pl.ds(1, 1)] = mixed[4:5]
        d_arrivals = []
        for o in sorted(range(1, depth), key=lambda o: -min(o, depth - o)):
            dest = shift(z, o, depth)
            copy = send(
                packed.at[dest], got_z.at[o], d_send.at[o], d_recv.at[o],
                at(zl_=lax.rem(dest, zls), zh_=dest // zls),
            )
            sends.append(copy)
            d_arrivals.append((o, copy))
        total = packed[z]
        for o, copy in reversed(d_arrivals):
            copy.wait_recv()
            total += got_z[o]
        for a in range(2):
            for b in range(4):
                corr_ref[pl.ds(4 * a + b, 1), :] = total[a : a + 1, b * width : (b + 1) * width]

        for copy in [one for pair in halos.values() for one in pair]:
            copy.wait_send()
        for copy in list(arrivals.values()) + sends:
            copy.wait_send()
        for copy in stores:
            copy.wait()

    return kernel


def solution(mesh):
    zls, zhs = 8, 4
    xs = mesh.shape["dom"] // (zls * CORES)
    ys = mesh.shape["grp"] // zhs
    stencil = plane_stencil()

    def shards(orbitals, potential):
        planes = jnp.transpose(orbitals, (1, 0, 2))
        count = planes.shape[1]
        dma = pltpu.SemaphoreType.DMA
        f32, bf16 = jnp.float32, jnp.bfloat16
        filtered, corr = pl.pallas_call(
            make_kernel(xs, zls, ys, zhs),
            out_shape=(
                jax.ShapeDtypeStruct((PLANES, count, CELLS), f32),
                jax.ShapeDtypeStruct((8, count), f32),
            ),
            in_specs=[pl.BlockSpec(memory_space=pl.ANY)] * 3,
            out_specs=(
                pl.BlockSpec(memory_space=pl.ANY),
                pl.BlockSpec(memory_space=pltpu.VMEM),
            ),
            scratch_shapes=[
                pltpu.VMEM((CHUNKS, PLANES, ROWS, CELLS), f32),
                pltpu.VMEM((CHUNKS, PLANES, ROWS, CELLS), f32),
                pltpu.VMEM((CELLS, CELLS), bf16),
                pltpu.VMEM((PLANES, CELLS), f32),
                pltpu.VMEM((PLANES, CELLS), f32),
                pltpu.VMEM((4, CHUNKS, 12, ROWS, CELLS), bf16),
                pltpu.VMEM((4, CHUNKS, 7, ROWS, CELLS), bf16),
                pltpu.VMEM((4, CHUNKS, 7, ROWS, CELLS), bf16),
                pltpu.VMEM((CHUNKS, zhs, 3, ROWS, 2 * LANES), bf16),
                pltpu.VMEM((CHUNKS, 3, ROWS, 2 * LANES), bf16),
                pltpu.VMEM((ys, zhs, CHUNKS, 3, ROWS, 2 * LANES), bf16),
                pltpu.VMEM((xs, CORES, zls // 2, 16, LANES), bf16),
                pltpu.VMEM((xs, CORES, zls // 2, 16, LANES), bf16),
                pltpu.VMEM((zls * zhs, 2, LANES), f32),
                pltpu.VMEM((zls * zhs, 2, LANES), f32),
                dma((4,)),
                dma((CHUNKS,)),
                pltpu.SemaphoreType.REGULAR,
                pltpu.SemaphoreType.REGULAR,
                dma((4, CHUNKS, PIECES, 2)),
                dma((4, CHUNKS, PIECES, 2)),
                dma((CHUNKS, 3)),
                dma((CHUNKS, 3)),
                dma((CHUNKS,)),
                dma((CHUNKS,)),
                dma((CHUNKS, 4, 3)),
                dma((CHUNKS, 4, 3)),
                dma((xs, CORES)),
                dma((xs, CORES)),
                dma((zls * zhs,)),
                dma((zls * zhs,)),
            ],
            compiler_params=pltpu.CompilerParams(
                collective_id=0, has_side_effects=True, vmem_limit_bytes=60 * 1024 * 1024
            ),
            cost_estimate=pl.CostEstimate(flops=10**9, bytes_accessed=1500000, transcendentals=0),
        )(planes, potential, jnp.asarray(stencil))
        return jnp.transpose(2.0 * filtered, (1, 0, 2)), jnp.transpose(corr, (1, 0)) * (1.0 / (NZ * CELLS))

    in_specs = (P("grp", "dom", None), P("dom", None))
    out_specs = (P("grp", "dom", None), P("grp", "dom"))
    return jax.shard_map(shards, mesh=mesh, in_specs=in_specs, out_specs=out_specs, check_vma=False)
```
